32 devices in a mesh: seq: 8 (over z, y), mp: 4 (over x, core).
Axes of the slice: x: 2, y: 2, z: 4, core: 2. Of those that a mesh axis runs over, the one named last changes fastest.
Arguments:
- query_states: bfloat16 [1024, 2048], P('seq', 'mp'), may hold values from -6 to 6
- key_states: bfloat16 [1024, 2048], P('seq', 'mp'), may hold values from -6 to 6
- value_states: bfloat16 [1024, 2048], P('seq', 'mp'), may hold values from -6 to 6
- lengths: int32 [8], replicated, may hold values from 32 to 128
- tokens: int32 [1024, 4], P('seq'), may hold values from 0 to 1023
- assignment: int32 [1024], P('seq'), may hold values from 0 to 2047, as said below
- proj_weight: bfloat16 [2048, 1024], P(('mp', 'seq')), may hold values from -0.5 to 0.5
- query_weight: bfloat16 [1024, 512], P('seq'), may hold values from -0.1875 to 0.1875
- key_weight: bfloat16 [1024, 512], P('seq'), may hold values from -0.1875 to 0.1875
- value_weight: bfloat16 [1024, 512], P('seq'), may hold values from -0.1875 to 0.1875
- out_weight: bfloat16 [512, 1024], P('seq'), may hold values from -0.25 to 0.25
- logit_weight: bfloat16 [1024, 1024], P('seq'), may hold values from -0.5 to 0.5
- embedding: bfloat16 [1024, 1024], P('seq'), may hold values from -6 to 6
- gain_attn: float32 [1024], replicated, may hold values from 0.1 to 1.9
- gain_head: float32 [1024], replicated, may hold values from 0.1 to 1.9
Outputs:
- context: bfloat16 [1024, 2048], P('seq', 'mp')
- context_grad: bfloat16 [1024, 2048], P('seq', 'mp')
- slot_loss: float32 [2048], P(('seq', 'mp'))
The draws below stay inside these ranges and needn't reach their ends.
Inputs may be any that keep to these rules, and one draw needn't show every extreme that they name: `assignment`: the frame with index f, on seq device s = f // 128, takes slot d * 256 + s * 32 + k for some depth group d and some 0 <= k < 32; no two frames share a slot.
All inputs are finite; a program needn't handle non-finite values.
Results may differ from the reference program's by a relative error of at most 0.028.
Values may be sent and summed in bfloat16 or wider, within the bound.
A program may use at most 64 MiB of HBM per device.

```python
import math
import jax
import jax.numpy as jnp
from jax import lax

D = 1024
HEAD_D = 64
HEAD_T = 128
VOCAB = 1024
CB = 4
FR_DEV = 128
CTXW = 2048
QW = 512
PAIR = 32
SLOTS = 2048
STREAM = 128
STREAMS = 8
FRAMES = 1024
N_SEQ = 8


def draw_assignment(key, part):
    key = jax.random.fold_in(key, 7)
    slot_cap = N_SEQ * PAIR
    hottest = jax.random.randint(jax.random.fold_in(key, 1), (), 0, N_SEQ)

    def one_source(source):
        source_key = jax.random.fold_in(jax.random.fold_in(key, 2), source)
        ranking = jax.random.permutation(jax.random.fold_in(source_key, 0), slot_cap)
        candidates = jnp.arange(slot_cap)
        scores = jnp.where(candidates // PAIR == hottest, -1 - candidates, ranking)
        picked = jnp.argsort(scores, stable=True)[:FR_DEV]
        shuffle = jax.random.permutation(jax.random.fold_in(source_key, 1), FR_DEV)
        chosen = picked[shuffle]
        return chosen // PAIR * slot_cap + source * PAIR + chosen % PAIR
    return jax.vmap(one_source)(jnp.arange(N_SEQ)).reshape(-1).astype(jnp.int32)


def plant(values, stream_key, least, top_value):
    dims = values.shape
    spot = [jax.random.randint(jax.random.fold_in(stream_key, axis), (), 0, dims[axis]) for axis in range(len(dims))]
    values = values.at[tuple(spot)].set(least)
    longest = dims.index(max(dims))
    spot[longest] = (spot[longest] + 1) % dims[longest]
    return values.at[tuple(spot)].set(top_value)


def steps_of(key, extent, shards, low, largest):
    level = 1.0
    for axis_at, parts in shards:
        steps = jax.random.uniform(jax.random.fold_in(jax.random.fold_in(key, 6), axis_at), (parts,), jnp.float32, low / len(shards), largest / len(shards))
        level = level * jnp.repeat(jnp.exp(steps), extent[axis_at] // parts).reshape((-1,) + (1,) * (len(extent) - 1 - axis_at))
    return level


def gaussian(stream_key, shape, deviation, reach, split=(), held_as=jnp.bfloat16):
    entries = jax.random.normal(stream_key, shape, jnp.float32) * deviation
    if len(split) > 0:
        entries = steps_of(stream_key, shape, split, -0.22, 0.18) * entries
    return jnp.clip(entries, min=-reach, max=reach).astype(held_as)


def setup_inputs(seed: int = 0) -> dict:
    streams_of = jax.random.split(jax.random.key(seed), 16)
    query_states = gaussian(streams_of[0], (FRAMES, CTXW), 1.0, 6.0, ((0, 8), (1, 4)))
    key_states = gaussian(streams_of[1], (FRAMES, CTXW), 1.0, 6.0, ((0, 8), (1, 4)))
    value_states = gaussian(streams_of[2], (FRAMES, CTXW), 1.0, 6.0, ((0, 8), (1, 4)))
    lengths = plant(jax.random.randint(streams_of[3], (STREAMS,), FR_DEV // 4, FR_DEV + 1), jax.random.fold_in(streams_of[3], 1), FR_DEV // 4, FR_DEV).astype(jnp.int32)
    tokens = plant(jax.random.randint(streams_of[4], (FRAMES, CB), 0, VOCAB), jax.random.fold_in(streams_of[4], 1), 0, VOCAB - 1).astype(jnp.int32)
    assignment = draw_assignment(jax.random.fold_in(streams_of[15], 71), 0)
    proj_weight = gaussian(streams_of[6], (CTXW, D), (CTXW // 16) ** -0.5, 0.5, ((0, 32),))
    query_weight = gaussian(streams_of[7], (D, QW), D ** -0.5, 0.1875, ((0, 8),))
    key_weight = gaussian(streams_of[8], (D, QW), D ** -0.5, 0.1875, ((0, 8),))
    value_weight = gaussian(streams_of[9], (D, QW), D ** -0.5, 0.1875, ((0, 8),))
    out_weight = gaussian(streams_of[10], (QW, D), QW ** -0.5, 0.25, ((0, 8),))
    logit_weight = gaussian(streams_of[11], (D, VOCAB), (D // 9) ** -0.5, 0.5, ((0, 8),))
    embedding = gaussian(streams_of[12], (VOCAB, D), 1.0, 6.0, ((0, 8),))
    gain_attn = jnp.clip(1.0 + 0.18 * jax.random.normal(streams_of[13], (D,), jnp.float32), 0.1, 1.9)
    gain_head = jnp.clip(1.0 + 0.18 * jax.random.normal(streams_of[14], (D,), jnp.float32), 0.1, 1.9)
    return dict(query_states=query_states, key_states=key_states, value_states=value_states, lengths=lengths, tokens=tokens, assignment=assignment, proj_weight=proj_weight, query_weight=query_weight, key_weight=key_weight, value_weight=value_weight, out_weight=out_weight, logit_weight=logit_weight, embedding=embedding, gain_attn=gain_attn, gain_head=gain_head)


NORM_EPS = 1e-05

def rms_scale(inputs, gain):
    return inputs * lax.rsqrt(lax.optimization_barrier(jnp.mean(inputs * inputs, axis=-1, keepdims=True)) + NORM_EPS) * gain.astype(jnp.float32)

def depth_losses(hidden, token_ids, live_mask, query_weight, key_weight, value_weight, out_weight, logit_weight, embedding, gain_attn, gain_head):
    frame_count = hidden.shape[0]
    model_width = hidden.shape[1]
    head_count = query_weight.shape[1] // HEAD_D
    row_count = frame_count * CB
    looked = jnp.take(embedding, token_ids[:, :CB - 1], axis=0).astype(jnp.float32)
    looked = jnp.concatenate([jnp.zeros((frame_count, 1, model_width), jnp.float32), looked], axis=1)
    inputs = hidden.astype(jnp.float32)[:, None, :] + looked
    normed = rms_scale(inputs, gain_attn).astype(jnp.bfloat16).reshape(row_count, model_width)
    head_shape = (frame_count, CB, head_count, HEAD_D)
    query_rows = jnp.dot(normed, query_weight, preferred_element_type=jnp.float32).astype(jnp.bfloat16).reshape(head_shape)
    key_rows = jnp.dot(normed, key_weight, preferred_element_type=jnp.float32).astype(jnp.bfloat16).reshape(head_shape)
    value_rows = jnp.dot(normed, value_weight, preferred_element_type=jnp.float32).astype(jnp.bfloat16).reshape(head_shape)
    scores = jnp.einsum('fqhd,fkhd->fhqk', query_rows, key_rows, preferred_element_type=jnp.float32) / math.sqrt(HEAD_D)
    places = jnp.arange(CB)
    causal = (places[None, :] <= places[:, None]).astype(jnp.float32)
    weights = jnp.exp(scores) * causal
    totals = lax.optimization_barrier(jnp.sum(weights, axis=-1))
    mixture = jnp.einsum('fhqk,fkhd->fqhd', weights.astype(jnp.bfloat16), value_rows, preferred_element_type=jnp.float32)
    mixture = mixture / jnp.transpose(totals, (0, 2, 1))[..., None]
    mixture = mixture.astype(jnp.bfloat16).reshape(row_count, head_count * HEAD_D)
    residual = inputs.reshape(row_count, model_width) + jnp.dot(mixture, out_weight, preferred_element_type=jnp.float32)
    head_in = rms_scale(residual, gain_head).astype(jnp.bfloat16)
    logits = jnp.dot(head_in, logit_weight, preferred_element_type=jnp.float32)
    log_total = jnp.log(lax.optimization_barrier(jnp.sum(jnp.exp(logits), axis=-1)))
    target = jnp.take_along_axis(logits, token_ids.reshape(row_count, 1), axis=1)[:, 0]
    per_frame = lax.optimization_barrier(jnp.sum((log_total - target).reshape(frame_count, CB), axis=1))
    return per_frame * live_mask

def stream_context(query_block, key_block, value_block, length):
    stream_rows = query_block.shape[0]
    head_count = query_block.shape[1] // HEAD_T
    head_shape = (stream_rows, head_count, HEAD_T)
    scores = jnp.einsum('qhd,khd->hqk', query_block.reshape(head_shape), key_block.reshape(head_shape), preferred_element_type=jnp.float32) / math.sqrt(HEAD_T)
    places = jnp.arange(stream_rows)
    causal = (places[None, :] <= places[:, None]).astype(jnp.float32)
    weights = jnp.exp(scores) * causal
    totals = lax.optimization_barrier(jnp.sum(weights, axis=-1))
    mixture = jnp.einsum('hqk,khd->qhd', weights.astype(jnp.bfloat16), value_block.reshape(head_shape), preferred_element_type=jnp.float32)
    mixture = mixture / jnp.transpose(totals)[:, :, None]
    live_mask = (places < length).astype(jnp.float32)
    return (mixture.reshape(stream_rows, -1) * live_mask[:, None]).astype(jnp.bfloat16)

def reference(query_states, key_states, value_states, lengths, tokens, assignment, proj_weight, query_weight, key_weight, value_weight, out_weight, logit_weight, embedding, gain_attn, gain_head):
    ctx_width = query_states.shape[1]
    stream_shape = (STREAMS, STREAM, ctx_width)
    context = lax.map(lambda block_parts: stream_context(*block_parts), (query_states.reshape(stream_shape), key_states.reshape(stream_shape), value_states.reshape(stream_shape), lengths)).reshape(FRAMES, ctx_width)
    places = jnp.arange(FRAMES)
    live_mask = (places % STREAM < lengths[places // STREAM]).astype(jnp.float32)

    def frame_block(block_parts):
        context_block, token_block, live_block = block_parts
        hidden = jnp.dot(context_block, proj_weight, preferred_element_type=jnp.float32).astype(jnp.bfloat16)

        def total_loss(hidden_in):
            per_frame = depth_losses(hidden_in, token_block, live_block, query_weight, key_weight, value_weight, out_weight, logit_weight, embedding, gain_attn, gain_head)
            return (jnp.sum(per_frame), per_frame)
        summed, pullback, per_frame = jax.vjp(total_loss, hidden, has_aux=True)
        hidden_grad = pullback(jnp.ones((), summed.dtype))[0]
        grad_block = jnp.dot(hidden_grad, proj_weight.T, preferred_element_type=jnp.float32).astype(jnp.bfloat16)
        return (grad_block, per_frame)
    grad_blocks, losses = lax.map(frame_block, (context.reshape(N_SEQ, FR_DEV, ctx_width), tokens.reshape(N_SEQ, FR_DEV, CB), live_mask.reshape(N_SEQ, FR_DEV)))
    slot_loss = jnp.zeros((SLOTS,), jnp.float32).at[assignment].set(losses.reshape(FRAMES))
    return (context, grad_blocks.reshape(FRAMES, ctx_width), slot_loss)
```

```python
import functools
import math

import jax
import jax.numpy as jnp
from jax import lax
from jax.experimental import pallas as pl
from jax.experimental.pallas import tpu as pltpu
from jax.sharding import PartitionSpec as P

HEAD_D = 64
HEAD_T = 128
CB = 4


NORM_EPS = 1e-05


def rms_scale(inputs, gain):
    return inputs * lax.rsqrt(jnp.mean(inputs * inputs, axis=-1, keepdims=True) + NORM_EPS) * gain


def depth_losses(
    hidden,
    token_ids,
    live_mask,
    query_weight,
    key_weight,
    value_weight,
    out_weight,
    logit_weight,
    embedding,
    gain_attn,
    gain_head,
):
    frame_count = hidden.shape[0]
    model_width = hidden.shape[1]
    head_count = query_weight.shape[1] // HEAD_D
    row_count = frame_count * CB
    looked = jnp.take(embedding, token_ids[:, : CB - 1], axis=0).astype(jnp.float32)
    looked = jnp.concatenate(
        [jnp.zeros((frame_count, 1, model_width), jnp.float32), looked], axis=1
    )
    inputs = hidden.astype(jnp.float32)[:, None, :] + looked
    normed = rms_scale(inputs, gain_attn).astype(jnp.bfloat16).reshape(row_count, model_width)
    head_shape = (frame_count, CB, head_count, HEAD_D)
    query_rows = (
        jnp.dot(normed, query_weight, preferred_element_type=jnp.float32)
        .astype(jnp.bfloat16)
        .reshape(head_shape)
    )
    key_rows = (
        jnp.dot(normed, key_weight, preferred_element_type=jnp.float32)
        .astype(jnp.bfloat16)
        .reshape(head_shape)
    )
    value_rows = (
        jnp.dot(normed, value_weight, preferred_element_type=jnp.float32)
        .astype(jnp.bfloat16)
        .reshape(head_shape)
    )
    scores = jnp.einsum(
        "fqhd,fkhd->fhqk", query_rows, key_rows, preferred_element_type=jnp.float32
    ) / math.sqrt(HEAD_D)
    places = jnp.arange(CB)
    causal = (places[None, :] <= places[:, None]).astype(jnp.float32)
    weights = jnp.exp(scores) * causal
    totals = jnp.sum(weights, axis=-1)
    mixture = jnp.einsum(
        "fhqk,fkhd->fqhd",
        weights.astype(jnp.bfloat16),
        value_rows,
        preferred_element_type=jnp.float32,
    )
    mixture = mixture / jnp.transpose(totals, (0, 2, 1))[..., None]
    mixture = mixture.astype(jnp.bfloat16).reshape(row_count, head_count * HEAD_D)
    residual = inputs.reshape(row_count, model_width) + jnp.dot(
        mixture, out_weight, preferred_element_type=jnp.float32
    )
    head_in = rms_scale(residual, gain_head).astype(jnp.bfloat16)
    logits = jnp.dot(head_in, logit_weight, preferred_element_type=jnp.float32)
    log_total = jnp.log(jnp.sum(jnp.exp(logits), axis=-1))
    target = jnp.take_along_axis(logits, token_ids.reshape(row_count, 1), axis=1)[:, 0]
    per_frame = jnp.sum((log_total - target).reshape(frame_count, CB), axis=1)
    return per_frame * live_mask


MESH = pl.DeviceIdType.MESH


def gather_kernel(line, *refs):
    count = (len(refs) - 3) // 2
    shards, wholes = refs[:count], refs[count : 2 * count]
    send_sem, recv_sem, local_sem = refs[2 * count :]
    seq, mp = lax.axis_index("seq"), lax.axis_index("mp")
    zi, yi = seq // 2, seq % 2
    xi, ci = mp // 2, mp % 2
    z_peers = [lax.rem(zi + d, line) * 2 + yi for d in range(1, line)]
    y_peer = zi * 2 + (1 - yi)
    x_peer = (1 - xi) * 2 + ci
    c_peer = xi * 2 + (1 - ci)

    barrier = pltpu.get_barrier_semaphore()
    greeted = [(peer, mp) for peer in z_peers] + [(y_peer, mp), (seq, x_peer), (seq, c_peer)]
    for peer in greeted:
        pl.semaphore_signal(barrier, inc=1, device_id=peer, device_id_type=MESH)
    pl.semaphore_wait(barrier, len(greeted))

    near = [lax.rem(zi + line - d, line) * 2 + yi for d in range(line)]
    far = [lax.rem(zi + line - d, line) * 2 + (1 - yi) for d in range(line)]
    others = near[1:] + far

    def rows_of(number, source, quarter):
        rows = shards[number].shape[0]
        if number == 0:
            return pl.ds(pl.multiple_of(source * rows, rows), rows)
        part = rows // 4
        return pl.ds(pl.multiple_of(source * rows + quarter * part, part), part)

    sends = []

    def send(number, rows, slot, peer, src=None):
        copy = pltpu.make_async_remote_copy(
            src_ref=wholes[number].at[rows, :] if src is None else src,
            dst_ref=wholes[number].at[rows, :],
            send_sem=send_sem.at[number, slot],
            recv_sem=recv_sem.at[number, slot],
            device_id=peer,
            device_id_type=MESH,
        )
        copy.start()
        sends.append(copy)

    def arrived(number, rows, slot):
        here = wholes[number].at[rows, :]
        pltpu.make_async_remote_copy(
            src_ref=here,
            dst_ref=here,
            send_sem=send_sem.at[number, slot],
            recv_sem=recv_sem.at[number, slot],
            device_id=(seq, mp),
            device_id_type=MESH,
        ).wait_recv()

    z_at = 0
    y_at = line - 1
    x_at = y_at + line
    c_at = x_at + 2 * line - 1
    xc_at = c_at + 2 * line - 1

    own_copies = []
    for number in range(count):
        rows = shards[number].shape[0]
        if number == 0:
            own = shards[number]
        else:
            part = rows // 4
            own = shards[number].at[pl.ds(pl.multiple_of(mp * part, part), part), :]
        target = rows_of(number, seq, mp)
        for d in range(1, line):
            send(number, target, z_at + d - 1, (z_peers[d - 1], mp), own)
        send(number, target, y_at, (y_peer, mp), own)
    for number in range(count):
        rows = shards[number].shape[0]
        copy = pltpu.make_async_copy(
            shards[number],
            wholes[number].at[pl.ds(pl.multiple_of(seq * rows, rows), rows), :],
            local_sem.at[number],
        )
        copy.start()
        own_copies.append(copy)

    def share(number, rows, at):
        if number > 0:
            send(number, rows, x_at + at, (seq, x_peer))
            send(number, rows, c_at + at, (seq, c_peer))

    def first_hops(number):
        for d in range(1, line):
            rows = rows_of(number, near[d], mp)
            arrived(number, rows, z_at + d - 1)
            send(number, rows, y_at + d, (y_peer, mp))
            share(number, rows, d - 1)
        for d in range(line):
            rows = rows_of(number, far[d], mp)
            arrived(number, rows, y_at + d)
            share(number, rows, line - 1 + d)

    def cross_hops(number):
        for at, source in enumerate(others):
            rows = rows_of(number, source, x_peer)
            arrived(number, rows, x_at + at)
            send(number, rows, xc_at + at, (seq, c_peer))

    for number in range(count):
        first_hops(number)
        if number > 1:
            cross_hops(number - 1)
    cross_hops(count - 1)
    diagonal = (1 - xi) * 2 + (1 - ci)
    for number in range(1, count):
        for at, source in enumerate(others):
            arrived(number, rows_of(number, source, c_peer), c_at + at)
            arrived(number, rows_of(number, source, diagonal), xc_at + at)
    for copy in own_copies:
        copy.wait()
    for copy in sends:
        copy.wait_send()


def gather_all(private, shared):
    seq_count = lax.axis_size("seq")
    shards = (private,) + shared
    small = private.shape[0] % 16 or any(part.shape[0] % 64 for part in shared)
    if small or seq_count != 8 or lax.axis_size("mp") != 4:
        return tuple(lax.all_gather(part, "seq", axis=0, tiled=True) for part in shards)
    line = seq_count // 2
    slots = (line - 1) + line + 3 * (2 * line - 1)
    count = len(shards)
    return pl.pallas_call(
        functools.partial(gather_kernel, line),
        out_shape=tuple(
            jax.ShapeDtypeStruct((part.shape[0] * seq_count, part.shape[1]), part.dtype)
            for part in shards
        ),
        in_specs=[pl.BlockSpec(memory_space=pl.ANY)] * count,
        out_specs=tuple([pl.BlockSpec(memory_space=pl.ANY)] * count),
        scratch_shapes=[
            pltpu.SemaphoreType.DMA((count, slots)),
            pltpu.SemaphoreType.DMA((count, slots)),
            pltpu.SemaphoreType.DMA((count,)),
        ],
        compiler_params=pltpu.CompilerParams(collective_id=0, has_side_effects=True),
    )(*shards)


def body(
    query_states,
    key_states,
    value_states,
    lengths,
    tokens,
    assignment,
    proj_weight,
    query_weight,
    key_weight,
    value_weight,
    out_weight,
    logit_weight,
    embedding,
    gain_attn,
    gain_head,
):
    seq_count = lax.axis_size("seq")
    seq_index = lax.axis_index("seq")
    frame_count = query_states.shape[0]
    local_width = query_states.shape[1]
    head_count = local_width // HEAD_T
    length = lengths[seq_index]
    places = jnp.arange(frame_count)
    visible = (places[None, :] <= places[:, None]).astype(jnp.float32)
    key_shape = (frame_count, head_count, HEAD_T)
    scores = jnp.einsum(
        "qhd,khd->hqk",
        query_states.reshape(key_shape),
        key_states.reshape(key_shape),
        preferred_element_type=jnp.float32,
    ) / math.sqrt(HEAD_T)
    weights = jnp.exp(scores) * visible[None, :, :]
    totals = jnp.sum(weights, axis=-1)
    mixture = jnp.einsum(
        "hqk,khd->qhd",
        weights.astype(jnp.bfloat16),
        value_states.reshape(key_shape),
        preferred_element_type=jnp.float32,
    )
    mixture = mixture / jnp.transpose(totals)[:, :, None]
    live_mask = (places < length).astype(jnp.float32)
    context = (mixture.reshape(frame_count, local_width) * live_mask[:, None]).astype(jnp.bfloat16)
    proj_quarter, embed_full, qkv_full, out_full, logit_full = gather_all(
        proj_weight,
        (
            embedding,
            jnp.concatenate([query_weight, key_weight, value_weight], axis=1),
            out_weight,
            logit_weight,
        ),
    )
    query_full, key_full, value_full = jnp.split(qkv_full, 3, axis=1)
    mp_count = lax.axis_size("mp")
    mp_index = lax.axis_index("mp")
    share = frame_count // mp_count
    first = mp_index * share
    partial_proj = jnp.dot(context, proj_quarter, preferred_element_type=jnp.float32)
    parts = lax.all_to_all(
        partial_proj.astype(jnp.bfloat16).reshape(mp_count, share, -1),
        "mp",
        split_axis=0,
        concat_axis=0,
    )
    hidden = jnp.sum(parts.astype(jnp.float32), axis=0).astype(jnp.bfloat16)
    own_tokens = lax.dynamic_slice_in_dim(tokens, first, share)
    own_live = lax.dynamic_slice_in_dim(live_mask, first, share)

    def total_loss(hidden_in):
        per_frame = depth_losses(
            hidden_in,
            own_tokens,
            own_live,
            query_full,
            key_full,
            value_full,
            out_full,
            logit_full,
            embed_full,
            gain_attn,
            gain_head,
        )
        return (jnp.sum(per_frame), per_frame)

    summed, pullback, own_loss = jax.vjp(total_loss, hidden, has_aux=True)
    hidden_grad = pullback(jnp.ones((), jnp.float32))[0]
    hidden_rows = lax.all_gather(hidden_grad, "mp", axis=0, tiled=True)
    context_grad = jnp.dot(hidden_rows, proj_quarter.T, preferred_element_type=jnp.float32).astype(
        jnp.bfloat16
    )
    frame_loss = lax.all_gather(own_loss, ("seq", "mp"), axis=0, tiled=True)
    frame_slot = lax.all_gather(assignment, "seq", axis=0, tiled=True)
    slot_count = 2 * share
    slots = (seq_index * mp_count + mp_index) * slot_count + jnp.arange(slot_count)
    slot_loss = jnp.sum(
        jnp.where(frame_slot[None, :] == slots[:, None], frame_loss[None, :], 0.0), axis=1
    )
    return (context, context_grad, slot_loss)


def solution(mesh):
    placed = (
        P("seq", "mp"),
        P("seq", "mp"),
        P("seq", "mp"),
        P(),
        P("seq", None),
        P("seq"),
        P(("mp", "seq"), None),
        P("seq", None),
        P("seq", None),
        P("seq", None),
        P("seq", None),
        P("seq", None),
        P("seq", None),
        P(),
        P(),
    )
    return jax.shard_map(
        body,
        mesh=mesh,
        in_specs=placed,
        out_specs=(P("seq", "mp"), P("seq", "mp"), P(("seq", "mp"))),
        check_vma=False,
    )
```

```python
import functools
import math

import jax
import jax.numpy as jnp
from jax import lax
from jax.experimental import pallas as pl
from jax.experimental.pallas import tpu as pltpu
from jax.sharding import PartitionSpec as P

HEAD_D = 64
HEAD_T = 128
CB = 4


NORM_EPS = 1e-05


def rms_scale(inputs, gain):
    return inputs * lax.rsqrt(jnp.mean(inputs * inputs, axis=-1, keepdims=True) + NORM_EPS) * gain


def depth_losses(
    hidden,
    token_ids,
    live_mask,
    query_weight,
    key_weight,
    value_weight,
    out_weight,
    logit_weight,
    embedding,
    gain_attn,
    gain_head,
):
    frame_count = hidden.shape[0]
    model_width = hidden.shape[1]
    head_count = query_weight.shape[1] // HEAD_D
    row_count = frame_count * CB
    looked = jnp.take(embedding, token_ids[:, : CB - 1], axis=0).astype(jnp.float32)
    looked = jnp.concatenate(
        [jnp.zeros((frame_count, 1, model_width), jnp.float32), looked], axis=1
    )
    inputs = hidden.astype(jnp.float32)[:, None, :] + looked
    normed = rms_scale(inputs, gain_attn).astype(jnp.bfloat16).reshape(row_count, model_width)
    head_shape = (frame_count, CB, head_count, HEAD_D)
    query_rows = (
        jnp.dot(normed, query_weight, preferred_element_type=jnp.float32)
        .astype(jnp.bfloat16)
        .reshape(head_shape)
    )
    key_rows = (
        jnp.dot(normed, key_weight, preferred_element_type=jnp.float32)
        .astype(jnp.bfloat16)
        .reshape(head_shape)
    )
    value_rows = (
        jnp.dot(normed, value_weight, preferred_element_type=jnp.float32)
        .astype(jnp.bfloat16)
        .reshape(head_shape)
    )
    scores = jnp.einsum(
        "fqhd,fkhd->fhqk", query_rows, key_rows, preferred_element_type=jnp.float32
    ) / math.sqrt(HEAD_D)
    places = jnp.arange(CB)
    causal = (places[None, :] <= places[:, None]).astype(jnp.float32)
    weights = jnp.exp(scores) * causal
    totals = jnp.sum(weights, axis=-1)
    mixture = jnp.einsum(
        "fhqk,fkhd->fqhd",
        weights.astype(jnp.bfloat16),
        value_rows,
        preferred_element_type=jnp.float32,
    )
    mixture = mixture / jnp.transpose(totals, (0, 2, 1))[..., None]
    mixture = mixture.astype(jnp.bfloat16).reshape(row_count, head_count * HEAD_D)
    residual = inputs.reshape(row_count, model_width) + jnp.dot(
        mixture, out_weight, preferred_element_type=jnp.float32
    )
    head_in = rms_scale(residual, gain_head).astype(jnp.bfloat16)
    logits = jnp.dot(head_in, logit_weight, preferred_element_type=jnp.float32)
    log_total = jnp.log(jnp.sum(jnp.exp(logits), axis=-1))
    target = jnp.take_along_axis(logits, token_ids.reshape(row_count, 1), axis=1)[:, 0]
    per_frame = jnp.sum((log_total - target).reshape(frame_count, CB), axis=1)
    return per_frame * live_mask


MESH = pl.DeviceIdType.MESH


PAIRS = [(c, k) for c in range(CB) for k in range(c + 1)]


def dot(left, right):
    return jnp.dot(left, right, preferred_element_type=jnp.float32)


def dot_turned(left, right):
    return lax.dot_general(left, right, (((1,), (1,)), ((), ())), preferred_element_type=jnp.float32)


def inverse_rms(rows):
    return lax.rsqrt(jnp.mean(rows * rows, axis=-1, keepdims=True) + NORM_EPS)


def rms_back(rows, scale, gain, grad):
    turned = grad * gain
    return scale * (turned - rows * (scale * scale) * jnp.mean(turned * rows, axis=-1, keepdims=True))


def slab(rows, place):
    size = rows.shape[0] // CB
    return rows[place * size : (place + 1) * size]


def head_sums(values):
    width = values.shape[1]
    left = lax.broadcasted_iota(jnp.int32, (width, width), 0) // HEAD_D
    right = lax.broadcasted_iota(jnp.int32, (width, width), 1) // HEAD_D
    ones = jnp.where(left == right, 1.0, 0.0).astype(jnp.bfloat16)
    high = values.astype(jnp.bfloat16)
    low = (values - high.astype(jnp.float32)).astype(jnp.bfloat16)
    return dot(high, ones) + dot(low, ones)


def temporal_head(query, key, value, live):
    size = query.shape[0]
    scores = dot_turned(query, key) / math.sqrt(HEAD_T)
    visible = lax.broadcasted_iota(jnp.int32, (size, size), 1) <= lax.broadcasted_iota(
        jnp.int32, (size, size), 0
    )
    weights = jnp.where(visible, jnp.exp(scores), 0.0)
    totals = jnp.sum(weights, axis=-1, keepdims=True)
    mixture = dot(weights.astype(jnp.bfloat16), value) / totals
    return (mixture * live).astype(jnp.bfloat16)


def chosen(ids, width):
    return lax.broadcasted_iota(jnp.int32, (ids.shape[0], width), 1) == ids


def depth_attention(qkv):
    width = qkv.shape[1] // 3
    query, key, value = (
        qkv[:, at * width : (at + 1) * width].astype(jnp.float32) for at in range(3)
    )
    products = jnp.concatenate([slab(query, c) * slab(key, k) for c, k in PAIRS], axis=0)
    weights = jnp.exp(head_sums(products) / math.sqrt(HEAD_D))
    size = products.shape[0] // len(PAIRS)
    parts = {pair: weights[at * size : (at + 1) * size] for at, pair in enumerate(PAIRS)}
    rounded = {
        pair: part.astype(jnp.bfloat16).astype(jnp.float32) for pair, part in parts.items()
    }
    totals = [sum(parts[c, k] for k in range(c + 1)) for c in range(CB)]
    mixed = [
        sum(rounded[c, k] * slab(value, k) for k in range(c + 1)) / totals[c] for c in range(CB)
    ]
    return jnp.concatenate(mixed, axis=0), (query, key, value, parts, rounded, totals)


def depth_attention_back(grad, mixed, saved):
    query, key, value, parts, rounded, totals = saved
    down = [slab(grad, c) / totals[c] for c in range(CB)]
    products = [down[c] * slab(value, k) for c, k in PAIRS]
    products += [down[c] * slab(mixed, c) for c in range(CB)]
    sums = head_sums(jnp.concatenate(products, axis=0))
    size = grad.shape[0] // CB
    pieces = [sums[at * size : (at + 1) * size] for at in range(len(products))]
    back = {}
    for at, (c, k) in enumerate(PAIRS):
        weight_grad = pieces[at].astype(jnp.bfloat16).astype(jnp.float32)
        back[c, k] = (weight_grad - pieces[len(PAIRS) + c]) * parts[c, k] / math.sqrt(HEAD_D)
    query_grad = [sum(back[c, k] * slab(key, k) for k in range(c + 1)) for c in range(CB)]
    key_grad = [sum(back[c, k] * slab(query, c) for c in range(k, CB)) for k in range(CB)]
    value_grad = [sum(rounded[c, k] * down[c] for c in range(k, CB)) for k in range(CB)]
    return jnp.concatenate(
        [jnp.concatenate(part, axis=0) for part in (query_grad, key_grad, value_grad)], axis=1
    ).astype(jnp.bfloat16)


def depth_inputs(hidden, before, embed, gain):
    looked = dot(jnp.where(chosen(before, embed.shape[0]), 1.0, 0.0).astype(jnp.bfloat16), embed)
    inputs = jnp.concatenate([hidden] * CB, axis=0) + looked
    scale = inverse_rms(inputs)
    return inputs, scale, (inputs * scale * gain).astype(jnp.bfloat16)


def depth_loss(head_in, ids, live, logit_weight):
    logits = dot(head_in, logit_weight)
    powers = jnp.exp(logits)
    total = jnp.sum(powers, axis=-1, keepdims=True)
    taken = chosen(ids, logits.shape[1])
    row_loss = jnp.log(total) - jnp.sum(jnp.where(taken, logits, 0.0), axis=-1, keepdims=True)
    frame_loss = sum(slab(row_loss, c) for c in range(CB)) * live
    live_rows = jnp.concatenate([live] * CB, axis=0)
    return frame_loss, (powers / total - jnp.where(taken, 1.0, 0.0)) * live_rows


def whole_kernel(line, bucket, *refs):
    (query, key, value, live, own_live, before, ids, places, gain_attn, gain_head) = refs[:10]
    private, query_shard, key_shard, value_shard, out_shard, logit_shard, embed_shard = refs[10:17]
    context, context_grad, losses = refs[17:20]
    wholes = refs[20:25]
    part_out, part_in, grads, loss_parts, loss_tiles = refs[25:30]
    send_sem, recv_sem, local_sem, swap_send, swap_recv, tile_send, tile_recv = refs[30:]
    proj_whole, embed_whole, qkv_whole, out_whole, logit_whole = wholes
    count = 5
    seq, mp = lax.axis_index("seq"), lax.axis_index("mp")
    seq_count = 2 * line
    zi, yi = seq // 2, seq % 2
    xi, ci = mp // 2, mp % 2
    z_peers = [lax.rem(zi + d, line) * 2 + yi for d in range(1, line)]
    y_peer = zi * 2 + (1 - yi)
    x_peer = (1 - xi) * 2 + ci
    c_peer = xi * 2 + (1 - ci)
    diagonal = (1 - xi) * 2 + (1 - ci)
    swap_peers = [c_peer, x_peer, diagonal]
    shard_rows = [whole.shape[0] // seq_count for whole in wholes]
    own = [
        pl.ds(pl.multiple_of(seq * rows, rows), rows) for rows in shard_rows
    ]
    width = query_shard.shape[1]

    locals_ = [
        (private, proj_whole.at[own[0], :]),
        (embed_shard, embed_whole.at[own[1], :]),
        (query_shard, qkv_whole.at[own[2], 0:width]),
        (key_shard, qkv_whole.at[own[2], width : 2 * width]),
        (value_shard, qkv_whole.at[own[2], 2 * width : 3 * width]),
        (out_shard, out_whole.at[own[3], :]),
        (logit_shard, logit_whole.at[own[4], :]),
    ]
    local_copies = [
        pltpu.make_async_copy(source, target, local_sem.at[at])
        for at, (source, target) in enumerate(locals_)
    ]
    for copy in local_copies:
        copy.start()

    barrier = pltpu.get_barrier_semaphore()
    greeted = [(lax.rem(seq + d, seq_count), mp) for d in range(1, seq_count)]
    greeted += [(seq, peer) for peer in swap_peers]
    for peer in greeted:
        pl.semaphore_signal(barrier, inc=1, device_id=peer, device_id_type=MESH)
    pl.semaphore_wait(barrier, len(greeted))
    for copy in local_copies:
        copy.wait()

    near = [lax.rem(zi + line - d, line) * 2 + yi for d in range(line)]
    far = [lax.rem(zi + line - d, line) * 2 + (1 - yi) for d in range(line)]
    others = near[1:] + far

    def rows_of(number, source, quarter):
        rows = shard_rows[number]
        if number == 0:
            return pl.ds(pl.multiple_of(source * rows, rows), rows)
        part = rows // 4
        return pl.ds(pl.multiple_of(source * rows + quarter * part, part), part)

    sends = []

    def remote(source, target, leaving, landing, peer):
        return pltpu.make_async_remote_copy(
            src_ref=source,
            dst_ref=target,
            send_sem=leaving,
            recv_sem=landing,
            device_id=peer,
            device_id_type=MESH,
        )

    def send(number, rows, slot, peer):
        here = wholes[number].at[rows, :]
        copy = remote(here, here, send_sem.at[number, slot], recv_sem.at[number, slot], peer)
        copy.start()
        sends.append(copy)

    def arrived(number, rows, slot):
        here = wholes[number].at[rows, :]
        remote(
            here, here, send_sem.at[number, slot], recv_sem.at[number, slot], (seq, c_peer)
        ).wait_recv()

    z_at = 0
    y_at = line - 1
    x_at = y_at + line
    c_at = x_at + 2 * line - 1
    xc_at = c_at + 2 * line - 1

    for number in range(count):
        target = rows_of(number, seq, mp)
        for d in range(1, line):
            send(number, target, z_at + d - 1, (z_peers[d - 1], mp))
        send(number, target, y_at, (y_peer, mp))

    def pass_on(number, rows, at):
        if number > 0:
            send(number, rows, x_at + at, (seq, x_peer))
            send(number, rows, c_at + at, (seq, c_peer))

    def first_hops(number):
        for d in range(1, line):
            rows = rows_of(number, near[d], mp)
            arrived(number, rows, z_at + d - 1)
            send(number, rows, y_at + d, (y_peer, mp))
            pass_on(number, rows, d - 1)
        for d in range(line):
            rows = rows_of(number, far[d], mp)
            arrived(number, rows, y_at + d)
            pass_on(number, rows, line - 1 + d)

    def cross_hops(number):
        for at, source in enumerate(others):
            rows = rows_of(number, source, x_peer)
            arrived(number, rows, x_at + at)
            send(number, rows, xc_at + at, (seq, c_peer))

    def finish(number):
        for at, source in enumerate(others):
            arrived(number, rows_of(number, source, c_peer), c_at + at)
            arrived(number, rows_of(number, source, diagonal), xc_at + at)

    for head in range(query.shape[1] // HEAD_T):
        columns = slice(head * HEAD_T, (head + 1) * HEAD_T)
        context[:, columns] = temporal_head(
            query[:, columns], key[:, columns], value[:, columns], live[...]
        )

    first_hops(0)
    share = part_in.shape[1]
    partial = dot(context[...], proj_whole[...]).astype(jnp.bfloat16)
    for part in range(CB):
        part_out[part] = partial[part * share : (part + 1) * share]
    for at, peer in enumerate(swap_peers):
        copy = remote(
            part_out.at[peer], part_in.at[at], swap_send.at[0, at], swap_recv.at[0, at], (seq, peer)
        )
        copy.start()
        sends.append(copy)

    first_hops(1)
    first_hops(2)
    cross_hops(1)
    hidden = part_out[mp].astype(jnp.float32)
    for at, peer in enumerate(swap_peers):
        remote(
            part_out.at[peer], part_in.at[at], swap_send.at[0, at], swap_recv.at[0, at], (seq, peer)
        ).wait_recv()
        hidden = hidden + part_in[at].astype(jnp.float32)
    hidden = hidden.astype(jnp.bfloat16).astype(jnp.float32)
    first_hops(3)
    cross_hops(2)
    finish(1)
    inputs, scale, normed = depth_inputs(hidden, before[...], embed_whole[...], gain_attn[...])
    first_hops(4)
    cross_hops(3)
    finish(2)
    qkv = dot(normed, qkv_whole[...]).astype(jnp.bfloat16)
    mixed, saved = depth_attention(qkv)
    cross_hops(4)
    finish(3)
    residual = inputs + dot(mixed.astype(jnp.bfloat16), out_whole[...])
    head_scale = inverse_rms(residual)
    head_in = (residual * head_scale * gain_head[...]).astype(jnp.bfloat16)
    finish(4)
    frame_loss, logit_grad = depth_loss(head_in, ids[...], own_live[...], logit_whole[...])

    spots = (seq_count, frame_loss.shape[0], loss_parts.shape[2])
    lanes = lax.broadcasted_iota(jnp.int32, spots, 2)
    spot = lax.broadcasted_iota(jnp.int32, spots, 0) * bucket + lanes
    hit = jnp.logical_and(spot == places[...][None, :, :], lanes < bucket)
    loss_parts[3] = jnp.sum(jnp.where(hit, frame_loss[None, :, :], 0.0), axis=1)
    for at, peer in enumerate(swap_peers):
        copy = remote(
            loss_parts.at[3], loss_parts.at[at], swap_send.at[1, at], swap_recv.at[1, at], (seq, peer)
        )
        copy.start()
        sends.append(copy)

    head_grad = dot_turned(logit_grad.astype(jnp.bfloat16), logit_whole[...])
    head_grad = head_grad.astype(jnp.bfloat16).astype(jnp.float32)
    residual_grad = rms_back(residual, head_scale, gain_head[...], head_grad)
    mixture_grad = dot_turned(residual_grad.astype(jnp.bfloat16), out_whole[...])
    mixture_grad = mixture_grad.astype(jnp.bfloat16).astype(jnp.float32)
    qkv_grad = depth_attention_back(mixture_grad, mixed, saved)
    normed_grad = dot_turned(qkv_grad, qkv_whole[...]).astype(jnp.bfloat16).astype(jnp.float32)
    inputs_grad = residual_grad + rms_back(inputs, scale, gain_attn[...], normed_grad)
    grads[mp] = sum(slab(inputs_grad, c) for c in range(CB)).astype(jnp.bfloat16)
    for at, peer in enumerate(swap_peers):
        copy = remote(
            grads.at[mp], grads.at[mp], swap_send.at[2, at], swap_recv.at[2, at], (seq, peer)
        )
        copy.start()
        sends.append(copy)

    for at, peer in enumerate(swap_peers):
        remote(
            loss_parts.at[3], loss_parts.at[at], swap_send.at[1, at], swap_recv.at[1, at], (seq, peer)
        ).wait_recv()
    loss_tiles[seq] = loss_parts[0] + loss_parts[1] + loss_parts[2] + loss_parts[3]
    for d in range(1, seq_count):
        copy = remote(
            loss_tiles.at[seq],
            loss_tiles.at[seq],
            tile_send.at[d - 1],
            tile_recv.at[d - 1],
            (lax.rem(seq + d, seq_count), mp),
        )
        copy.start()
        sends.append(copy)

    for at, peer in enumerate(swap_peers):
        remote(
            grads.at[peer], grads.at[peer], swap_send.at[2, at], swap_recv.at[2, at], (seq, peer)
        ).wait_recv()
    rows = jnp.concatenate([grads[part] for part in range(CB)], axis=0)
    context_grad[...] = dot_turned(rows, proj_whole[...]).astype(jnp.bfloat16)
    for d in range(1, seq_count):
        source = lax.rem(seq + seq_count - d, seq_count)
        remote(
            loss_tiles.at[source],
            loss_tiles.at[source],
            tile_send.at[d - 1],
            tile_recv.at[d - 1],
            (source, mp),
        ).wait_recv()
    losses[...] = loss_tiles[...]
    for copy in sends:
        copy.wait_send()


def whole_step(
    query_states,
    key_states,
    value_states,
    lengths,
    tokens,
    assignment,
    proj_weight,
    query_weight,
    key_weight,
    value_weight,
    out_weight,
    logit_weight,
    embedding,
    gain_attn,
    gain_head,
):
    seq_count, mp_count = lax.axis_size("seq"), lax.axis_size("mp")
    seq_index, mp_index = lax.axis_index("seq"), lax.axis_index("mp")
    frame_count, local_width = query_states.shape
    share = frame_count // mp_count
    slot_cap = 2 * frame_count
    bucket = slot_cap // seq_count
    model_width = proj_weight.shape[1]
    first = mp_index * share
    live = (jnp.arange(frame_count) < lengths[seq_index]).astype(jnp.float32)[:, None]
    own_tokens = lax.dynamic_slice_in_dim(tokens, first, share).T
    none = jnp.full((1, share), -1, jnp.int32)
    before = jnp.concatenate([none, own_tokens[: CB - 1]], axis=0).reshape(-1, 1)
    places = assignment // slot_cap * bucket + assignment % slot_cap - seq_index * bucket
    line = seq_count // 2
    slots = (line - 1) + line + 3 * (2 * line - 1)
    vmem = pl.BlockSpec(memory_space=pltpu.VMEM)
    shard = pl.BlockSpec(memory_space=pl.ANY)
    depth_width = 3 * query_weight.shape[1]
    context, context_grad, tiles = pl.pallas_call(
        functools.partial(whole_kernel, line, bucket),
        out_shape=(
            jax.ShapeDtypeStruct((frame_count, local_width), jnp.bfloat16),
            jax.ShapeDtypeStruct((frame_count, local_width), jnp.bfloat16),
            jax.ShapeDtypeStruct((seq_count, seq_count, 128), jnp.float32),
        ),
        in_specs=[vmem] * 10 + [shard] * 7,
        out_specs=(vmem, vmem, vmem),
        scratch_shapes=[
            pltpu.VMEM((proj_weight.shape[0] * seq_count, model_width), jnp.bfloat16),
            pltpu.VMEM((embedding.shape[0] * seq_count, model_width), jnp.bfloat16),
            pltpu.VMEM((query_weight.shape[0] * seq_count, depth_width), jnp.bfloat16),
            pltpu.VMEM((out_weight.shape[0] * seq_count, model_width), jnp.bfloat16),
            pltpu.VMEM((logit_weight.shape[0] * seq_count, logit_weight.shape[1]), jnp.bfloat16),
            pltpu.VMEM((mp_count, share, model_width), jnp.bfloat16),
            pltpu.VMEM((mp_count - 1, share, model_width), jnp.bfloat16),
            pltpu.VMEM((mp_count, share, model_width), jnp.bfloat16),
            pltpu.VMEM((mp_count, seq_count, 128), jnp.float32),
            pltpu.VMEM((seq_count, seq_count, 128), jnp.float32),
            pltpu.SemaphoreType.DMA((5, slots)),
            pltpu.SemaphoreType.DMA((5, slots)),
            pltpu.SemaphoreType.DMA((7,)),
            pltpu.SemaphoreType.DMA((3, mp_count - 1)),
            pltpu.SemaphoreType.DMA((3, mp_count - 1)),
            pltpu.SemaphoreType.DMA((seq_count - 1,)),
            pltpu.SemaphoreType.DMA((seq_count - 1,)),
        ],
        compiler_params=pltpu.CompilerParams(
            collective_id=0, has_side_effects=True, vmem_limit_bytes=48 * 1024 * 1024
        ),
    )(
        query_states,
        key_states,
        value_states,
        live,
        lax.dynamic_slice_in_dim(live, first, share),
        before,
        own_tokens.reshape(-1, 1),
        lax.dynamic_slice_in_dim(places, first, share)[:, None],
        gain_attn[None, :],
        gain_head[None, :],
        proj_weight,
        query_weight,
        key_weight,
        value_weight,
        out_weight,
        logit_weight,
        embedding,
    )
    sources = slot_cap // mp_count // bucket
    mine = lax.dynamic_slice(
        tiles, (mp_index * sources, seq_index, 0), (sources, 1, bucket)
    )
    return (context, context_grad, mine.reshape(-1))


def fits(query_states, proj_weight, embedding, out_weight):
    seq_count = lax.axis_size("seq")
    return (
        seq_count == 8
        and lax.axis_size("mp") == 4
        and query_states.shape[0] % 128 == 0
        and proj_weight.shape[0] % 16 == 0
        and embedding.shape[0] % 64 == 0
        and out_weight.shape[0] % 64 == 0
    )


def gather_all(*shards):
    return tuple(lax.all_gather(part, "seq", axis=0, tiled=True) for part in shards)


def body(
    query_states,
    key_states,
    value_states,
    lengths,
    tokens,
    assignment,
    proj_weight,
    query_weight,
    key_weight,
    value_weight,
    out_weight,
    logit_weight,
    embedding,
    gain_attn,
    gain_head,
):
    if fits(query_states, proj_weight, embedding, out_weight):
        return whole_step(
            query_states,
            key_states,
            value_states,
            lengths,
            tokens,
            assignment,
            proj_weight,
            query_weight,
            key_weight,
            value_weight,
            out_weight,
            logit_weight,
            embedding,
            gain_attn,
            gain_head,
        )
    seq_index = lax.axis_index("seq")
    frame_count = query_states.shape[0]
    local_width = query_states.shape[1]
    head_count = local_width // HEAD_T
    length = lengths[seq_index]
    places = jnp.arange(frame_count)
    visible = (places[None, :] <= places[:, None]).astype(jnp.float32)
    key_shape = (frame_count, head_count, HEAD_T)
    scores = jnp.einsum(
        "qhd,khd->hqk",
        query_states.reshape(key_shape),
        key_states.reshape(key_shape),
        preferred_element_type=jnp.float32,
    ) / math.sqrt(HEAD_T)
    weights = jnp.exp(scores) * visible[None, :, :]
    totals = jnp.sum(weights, axis=-1)
    mixture = jnp.einsum(
        "hqk,khd->qhd",
        weights.astype(jnp.bfloat16),
        value_states.reshape(key_shape),
        preferred_element_type=jnp.float32,
    )
    mixture = mixture / jnp.transpose(totals)[:, :, None]
    live_mask = (places < length).astype(jnp.float32)
    context = (mixture.reshape(frame_count, local_width) * live_mask[:, None]).astype(jnp.bfloat16)
    proj_quarter, embed_full, qkv_full, out_full, logit_full = gather_all(
        proj_weight,
        embedding,
        jnp.concatenate([query_weight, key_weight, value_weight], axis=1),
        out_weight,
        logit_weight,
    )
    query_full, key_full, value_full = jnp.split(qkv_full, 3, axis=1)
    mp_count = lax.axis_size("mp")
    mp_index = lax.axis_index("mp")
    share = frame_count // mp_count
    first = mp_index * share
    partial_proj = jnp.dot(context, proj_quarter, preferred_element_type=jnp.float32)
    parts = lax.all_to_all(
        partial_proj.astype(jnp.bfloat16).reshape(mp_count, share, -1),
        "mp",
        split_axis=0,
        concat_axis=0,
    )
    hidden = jnp.sum(parts.astype(jnp.float32), axis=0).astype(jnp.bfloat16)
    own_tokens = lax.dynamic_slice_in_dim(tokens, first, share)
    own_live = lax.dynamic_slice_in_dim(live_mask, first, share)

    def total_loss(hidden_in):
        per_frame = depth_losses(
            hidden_in,
            own_tokens,
            own_live,
            query_full,
            key_full,
            value_full,
            out_full,
            logit_full,
            embed_full,
            gain_attn,
            gain_head,
        )
        return (jnp.sum(per_frame), per_frame)

    summed, pullback, own_loss = jax.vjp(total_loss, hidden, has_aux=True)
    hidden_grad = pullback(jnp.ones((), jnp.float32))[0]
    hidden_rows = lax.all_gather(hidden_grad, "mp", axis=0, tiled=True)
    context_grad = jnp.dot(hidden_rows, proj_quarter.T, preferred_element_type=jnp.float32).astype(
        jnp.bfloat16
    )
    frame_loss = lax.all_gather(own_loss, ("seq", "mp"), axis=0, tiled=True)
    frame_slot = lax.all_gather(assignment, "seq", axis=0, tiled=True)
    slot_count = 2 * share
    slots = (seq_index * mp_count + mp_index) * slot_count + jnp.arange(slot_count)
    slot_loss = jnp.sum(
        jnp.where(frame_slot[None, :] == slots[:, None], frame_loss[None, :], 0.0), axis=1
    )
    return (context, context_grad, slot_loss)


def solution(mesh):
    placed = (
        P("seq", "mp"),
        P("seq", "mp"),
        P("seq", "mp"),
        P(),
        P("seq", None),
        P("seq"),
        P(("mp", "seq"), None),
        P("seq", None),
        P("seq", None),
        P("seq", None),
        P("seq", None),
        P("seq", None),
        P("seq", None),
        P(),
        P(),
    )
    return jax.shard_map(
        body,
        mesh=mesh,
        in_specs=placed,
        out_specs=(P("seq", "mp"), P("seq", "mp"), P(("seq", "mp"))),
        check_vma=False,
    )
```

```python
import functools
import math

import jax
import jax.numpy as jnp
from jax import lax
from jax.experimental import pallas as pl
from jax.experimental.pallas import tpu as pltpu
from jax.sharding import PartitionSpec as P

HEAD_D = 64
HEAD_T = 128
CB = 4


NORM_EPS = 1e-05


def rms_scale(inputs, gain):
    return inputs * lax.rsqrt(jnp.mean(inputs * inputs, axis=-1, keepdims=True) + NORM_EPS) * gain


def depth_losses(
    hidden,
    token_ids,
    live_mask,
    query_weight,
    key_weight,
    value_weight,
    out_weight,
    logit_weight,
    embedding,
    gain_attn,
    gain_head,
):
    frame_count = hidden.shape[0]
    model_width = hidden.shape[1]
    head_count = query_weight.shape[1] // HEAD_D
    row_count = frame_count * CB
    looked = jnp.take(embedding, token_ids[:, : CB - 1], axis=0).astype(jnp.float32)
    looked = jnp.concatenate(
        [jnp.zeros((frame_count, 1, model_width), jnp.float32), looked], axis=1
    )
    inputs = hidden.astype(jnp.float32)[:, None, :] + looked
    normed = rms_scale(inputs, gain_attn).astype(jnp.bfloat16).reshape(row_count, model_width)
    head_shape = (frame_count, CB, head_count, HEAD_D)
    query_rows = (
        jnp.dot(normed, query_weight, preferred_element_type=jnp.float32)
        .astype(jnp.bfloat16)
        .reshape(head_shape)
    )
    key_rows = (
        jnp.dot(normed, key_weight, preferred_element_type=jnp.float32)
        .astype(jnp.bfloat16)
        .reshape(head_shape)
    )
    value_rows = (
        jnp.dot(normed, value_weight, preferred_element_type=jnp.float32)
        .astype(jnp.bfloat16)
        .reshape(head_shape)
    )
    scores = jnp.einsum(
        "fqhd,fkhd->fhqk", query_rows, key_rows, preferred_element_type=jnp.float32
    ) / math.sqrt(HEAD_D)
    places = jnp.arange(CB)
    causal = (places[None, :] <= places[:, None]).astype(jnp.float32)
    weights = jnp.exp(scores) * causal
    totals = jnp.sum(weights, axis=-1)
    mixture = jnp.einsum(
        "fhqk,fkhd->fqhd",
        weights.astype(jnp.bfloat16),
        value_rows,
        preferred_element_type=jnp.float32,
    )
    mixture = mixture / jnp.transpose(totals, (0, 2, 1))[..., None]
    mixture = mixture.astype(jnp.bfloat16).reshape(row_count, head_count * HEAD_D)
    residual = inputs.reshape(row_count, model_width) + jnp.dot(
        mixture, out_weight, preferred_element_type=jnp.float32
    )
    head_in = rms_scale(residual, gain_head).astype(jnp.bfloat16)
    logits = jnp.dot(head_in, logit_weight, preferred_element_type=jnp.float32)
    log_total = jnp.log(jnp.sum(jnp.exp(logits), axis=-1))
    target = jnp.take_along_axis(logits, token_ids.reshape(row_count, 1), axis=1)[:, 0]
    per_frame = jnp.sum((log_total - target).reshape(frame_count, CB), axis=1)
    return per_frame * live_mask


MESH = pl.DeviceIdType.MESH


ORDER = (1, 0, 2, 3, 4)
AHEAD = 2
PAIRS = [(c, k) for c in range(CB) for k in range(c + 1)]


def dot(left, right):
    return jnp.dot(left, right, preferred_element_type=jnp.float32)


def dot_turned(left, right):
    return lax.dot_general(left, right, (((1,), (1,)), ((), ())), preferred_element_type=jnp.float32)


def inverse_rms(rows):
    return lax.rsqrt(jnp.mean(rows * rows, axis=-1, keepdims=True) + NORM_EPS)


def rms_back(rows, scale, gain, grad):
    turned = grad * gain
    return scale * (turned - rows * (scale * scale) * jnp.mean(turned * rows, axis=-1, keepdims=True))


def slab(rows, place):
    size = rows.shape[0] // CB
    return rows[place * size : (place + 1) * size]


def head_sums(values):
    width = values.shape[1]
    left = lax.broadcasted_iota(jnp.int32, (width, width), 0) // HEAD_D
    right = lax.broadcasted_iota(jnp.int32, (width, width), 1) // HEAD_D
    ones = jnp.where(left == right, 1.0, 0.0).astype(jnp.bfloat16)
    high = values.astype(jnp.bfloat16)
    low = (values - high.astype(jnp.float32)).astype(jnp.bfloat16)
    return dot(high, ones) + dot(low, ones)


def temporal_head(query, key, value, live):
    size = query.shape[0]
    scores = dot_turned(query, key) / math.sqrt(HEAD_T)
    visible = lax.broadcasted_iota(jnp.int32, (size, size), 1) <= lax.broadcasted_iota(
        jnp.int32, (size, size), 0
    )
    weights = jnp.where(visible, jnp.exp(scores), 0.0)
    totals = jnp.sum(weights, axis=-1, keepdims=True)
    mixture = dot(weights.astype(jnp.bfloat16), value) / totals
    return (mixture * live).astype(jnp.bfloat16)


def chosen(ids, width):
    return lax.broadcasted_iota(jnp.int32, (ids.shape[0], width), 1) == ids


def depth_attention(qkv):
    width = qkv.shape[1] // 3
    query, key, value = (
        qkv[:, at * width : (at + 1) * width].astype(jnp.float32) for at in range(3)
    )
    products = jnp.concatenate([slab(query, c) * slab(key, k) for c, k in PAIRS], axis=0)
    weights = jnp.exp(head_sums(products) / math.sqrt(HEAD_D))
    size = products.shape[0] // len(PAIRS)
    parts = {pair: weights[at * size : (at + 1) * size] for at, pair in enumerate(PAIRS)}
    rounded = {
        pair: part.astype(jnp.bfloat16).astype(jnp.float32) for pair, part in parts.items()
    }
    totals = [sum(parts[c, k] for k in range(c + 1)) for c in range(CB)]
    mixed = [
        sum(rounded[c, k] * slab(value, k) for k in range(c + 1)) / totals[c] for c in range(CB)
    ]
    return jnp.concatenate(mixed, axis=0), (query, key, value, parts, rounded, totals)


def depth_attention_back(grad, mixed, saved):
    query, key, value, parts, rounded, totals = saved
    down = [slab(grad, c) / totals[c] for c in range(CB)]
    products = [down[c] * slab(value, k) for c, k in PAIRS]
    products += [down[c] * slab(mixed, c) for c in range(CB)]
    sums = head_sums(jnp.concatenate(products, axis=0))
    size = grad.shape[0] // CB
    pieces = [sums[at * size : (at + 1) * size] for at in range(len(products))]
    back = {}
    for at, (c, k) in enumerate(PAIRS):
        weight_grad = pieces[at].astype(jnp.bfloat16).astype(jnp.float32)
        back[c, k] = (weight_grad - pieces[len(PAIRS) + c]) * parts[c, k] / math.sqrt(HEAD_D)
    query_grad = [sum(back[c, k] * slab(key, k) for k in range(c + 1)) for c in range(CB)]
    key_grad = [sum(back[c, k] * slab(query, c) for c in range(k, CB)) for k in range(CB)]
    value_grad = [sum(rounded[c, k] * down[c] for c in range(k, CB)) for k in range(CB)]
    return jnp.concatenate(
        [jnp.concatenate(part, axis=0) for part in (query_grad, key_grad, value_grad)], axis=1
    ).astype(jnp.bfloat16)


def depth_inputs(hidden, before, embed, gain):
    looked = dot(jnp.where(chosen(before, embed.shape[0]), 1.0, 0.0).astype(jnp.bfloat16), embed)
    inputs = jnp.concatenate([hidden] * CB, axis=0) + looked
    scale = inverse_rms(inputs)
    return inputs, scale, (inputs * scale * gain).astype(jnp.bfloat16)


def depth_loss(head_in, ids, live, logit_weight):
    logits = dot(head_in, logit_weight)
    powers = jnp.exp(logits)
    total = jnp.sum(powers, axis=-1, keepdims=True)
    taken = chosen(ids, logits.shape[1])
    row_loss = jnp.log(total) - jnp.sum(jnp.where(taken, logits, 0.0), axis=-1, keepdims=True)
    frame_loss = sum(slab(row_loss, c) for c in range(CB)) * live
    live_rows = jnp.concatenate([live] * CB, axis=0)
    return frame_loss, (powers / total - jnp.where(taken, 1.0, 0.0)) * live_rows


def whole_kernel(line, bucket, *refs):
    lengths, tokens, assignment, gain_attn, gain_head = refs[:5]
    query_states, key_states, value_states = refs[5:8]
    private, query_shard, key_shard, value_shard, out_shard, logit_shard, embed_shard = refs[8:15]
    context, context_grad, losses = refs[15:18]
    wholes = refs[18:23]
    part_out, part_in, grads, loss_parts, loss_tiles, query, key, value = refs[23:31]
    send_sem, recv_sem, local_sem, swap_send, swap_recv, tile_send, tile_recv = refs[31:]
    proj_whole, embed_whole, qkv_whole, out_whole, logit_whole = wholes
    count = 5
    seq, mp = lax.axis_index("seq"), lax.axis_index("mp")
    seq_count = 2 * line
    zi, yi = seq // 2, seq % 2
    xi, ci = mp // 2, mp % 2
    z_peers = [lax.rem(zi + d, line) * 2 + yi for d in range(1, line)]
    y_peer = zi * 2 + (1 - yi)
    x_peer = (1 - xi) * 2 + ci
    c_peer = xi * 2 + (1 - ci)
    diagonal = (1 - xi) * 2 + (1 - ci)
    swap_peers = [c_peer, x_peer, diagonal]
    shard_rows = [whole.shape[0] // seq_count for whole in wholes]
    own = [
        pl.ds(pl.multiple_of(seq * rows, rows), rows) for rows in shard_rows
    ]
    width = query_shard.shape[1]

    locals_ = [
        (private, proj_whole.at[own[0], :]),
        (embed_shard, embed_whole.at[own[1], :]),
        (query_shard, qkv_whole.at[own[2], 0:width]),
        (key_shard, qkv_whole.at[own[2], width : 2 * width]),
        (value_shard, qkv_whole.at[own[2], 2 * width : 3 * width]),
        (out_shard, out_whole.at[own[3], :]),
        (logit_shard, logit_whole.at[own[4], :]),
        (query_states, query),
        (key_states, key),
        (value_states, value),
    ]
    local_copies = [
        pltpu.make_async_copy(source, target, local_sem.at[at])
        for at, (source, target) in enumerate(locals_)
    ]
    for copy in local_copies:
        copy.start()

    barrier = pltpu.get_barrier_semaphore()
    greeted = [(lax.rem(seq + d, seq_count), mp) for d in range(1, seq_count)]
    greeted += [(seq, peer) for peer in swap_peers]
    for peer in greeted:
        pl.semaphore_signal(barrier, inc=1, device_id=peer, device_id_type=MESH)
    pl.semaphore_wait(barrier, len(greeted))
    for copy in local_copies[:7]:
        copy.wait()

    near = [lax.rem(zi + line - d, line) * 2 + yi for d in range(line)]
    far = [lax.rem(zi + line - d, line) * 2 + (1 - yi) for d in range(line)]
    others = near[1:] + far

    def rows_of(number, source, quarter):
        rows = shard_rows[number]
        if number == 0:
            return pl.ds(pl.multiple_of(source * rows, rows), rows)
        part = rows // 4
        return pl.ds(pl.multiple_of(source * rows + quarter * part, part), part)

    sends = []

    def remote(source, target, leaving, landing, peer):
        return pltpu.make_async_remote_copy(
            src_ref=source,
            dst_ref=target,
            send_sem=leaving,
            recv_sem=landing,
            device_id=peer,
            device_id_type=MESH,
        )

    def send(number, rows, slot, peer):
        here = wholes[number].at[rows, :]
        copy = remote(here, here, send_sem.at[number, slot], recv_sem.at[number, slot], peer)
        copy.start()
        sends.append(copy)

    def arrived(number, rows, slot):
        here = wholes[number].at[rows, :]
        remote(
            here, here, send_sem.at[number, slot], recv_sem.at[number, slot], (seq, c_peer)
        ).wait_recv()

    z_at = 0
    y_at = line - 1
    x_at = y_at + line
    c_at = x_at + 2 * line - 1
    xc_at = c_at + 2 * line - 1

    def own_sends(number):
        target = rows_of(number, seq, mp)
        send(number, target, y_at, (y_peer, mp))
        for d in range(1, line):
            send(number, target, z_at + d - 1, (z_peers[d - 1], mp))

    for number in ORDER[:AHEAD]:
        own_sends(number)

    def pass_on(number, rows, at):
        if number > 0:
            send(number, rows, x_at + at, (seq, x_peer))
            send(number, rows, c_at + at, (seq, c_peer))

    def first_hops(number):
        later = ORDER.index(number) + AHEAD
        if later < count:
            own_sends(ORDER[later])
        for d in range(line):
            if d > 0:
                rows = rows_of(number, near[d], mp)
                arrived(number, rows, z_at + d - 1)
                send(number, rows, y_at + d, (y_peer, mp))
                pass_on(number, rows, d - 1)
            rows = rows_of(number, far[d], mp)
            arrived(number, rows, y_at + d)
            pass_on(number, rows, line - 1 + d)

    def cross_hops(number):
        for at, source in enumerate(others):
            rows = rows_of(number, source, x_peer)
            arrived(number, rows, x_at + at)
            send(number, rows, xc_at + at, (seq, c_peer))

    def finish(number):
        for at, source in enumerate(others):
            arrived(number, rows_of(number, source, c_peer), c_at + at)
            arrived(number, rows_of(number, source, diagonal), xc_at + at)

    for copy in local_copies[7:]:
        copy.wait()
    frames = query.shape[0]
    length = lengths[seq]
    live = jnp.where(
        lax.broadcasted_iota(jnp.int32, (frames, 1), 0) < length, 1.0, 0.0
    )
    for head in range(query.shape[1] // HEAD_T):
        columns = slice(head * HEAD_T, (head + 1) * HEAD_T)
        context[:, columns] = temporal_head(
            query[:, columns], key[:, columns], value[:, columns], live
        )

    for number in ORDER[:2]:
        first_hops(number)
    share = part_in.shape[1]
    partial = dot(context[...], proj_whole[...]).astype(jnp.bfloat16)
    for part in range(CB):
        part_out[part] = partial[part * share : (part + 1) * share]
    for at, peer in enumerate(swap_peers):
        copy = remote(
            part_out.at[peer], part_in.at[at], swap_send.at[0, at], swap_recv.at[0, at], (seq, peer)
        )
        copy.start()
        sends.append(copy)

    cross_hops(1)
    first_hops(2)
    first = pl.multiple_of(mp * share, share)
    own_tokens = tokens[pl.ds(first, share), :]
    columns = [own_tokens[:, c : c + 1] for c in range(CB)]
    ids = jnp.concatenate(columns, axis=0)
    before = jnp.concatenate([jnp.full((share, 1), -1, jnp.int32)] + columns[:-1], axis=0)
    frame = first + lax.broadcasted_iota(jnp.int32, (share, 1), 0)
    own_live = jnp.where(frame < length, 1.0, 0.0)
    own_frame = lax.broadcasted_iota(jnp.int32, (share, frames), 1) == frame
    slot = jnp.sum(jnp.where(own_frame, assignment[...], 0), axis=1, keepdims=True)
    slot_cap = bucket * seq_count
    places = slot // slot_cap * bucket + slot % slot_cap - seq * bucket
    hidden = part_out[mp].astype(jnp.float32)
    for at, peer in enumerate(swap_peers):
        remote(
            part_out.at[peer], part_in.at[at], swap_send.at[0, at], swap_recv.at[0, at], (seq, peer)
        ).wait_recv()
        hidden = hidden + part_in[at].astype(jnp.float32)
    hidden = hidden.astype(jnp.bfloat16).astype(jnp.float32)
    first_hops(3)
    cross_hops(2)
    finish(1)
    inputs, scale, normed = depth_inputs(hidden, before, embed_whole[...], gain_attn[...])
    first_hops(4)
    cross_hops(3)
    finish(2)
    qkv = dot(normed, qkv_whole[...]).astype(jnp.bfloat16)
    mixed, saved = depth_attention(qkv)
    cross_hops(4)
    finish(3)
    residual = inputs + dot(mixed.astype(jnp.bfloat16), out_whole[...])
    head_scale = inverse_rms(residual)
    head_in = (residual * head_scale * gain_head[...]).astype(jnp.bfloat16)
    finish(4)
    frame_loss, logit_grad = depth_loss(head_in, ids, own_live, logit_whole[...])

    spots = (seq_count, frame_loss.shape[0], loss_parts.shape[2])
    lanes = lax.broadcasted_iota(jnp.int32, spots, 2)
    spot = lax.broadcasted_iota(jnp.int32, spots, 0) * bucket + lanes
    hit = jnp.logical_and(spot == places[None, :, :], lanes < bucket)
    loss_parts[3] = jnp.sum(jnp.where(hit, frame_loss[None, :, :], 0.0), axis=1)
    for at, peer in enumerate(swap_peers):
        copy = remote(
            loss_parts.at[3], loss_parts.at[at], swap_send.at[1, at], swap_recv.at[1, at], (seq, peer)
        )
        copy.start()
        sends.append(copy)

    head_grad = dot_turned(logit_grad.astype(jnp.bfloat16), logit_whole[...])
    head_grad = head_grad.astype(jnp.bfloat16).astype(jnp.float32)
    residual_grad = rms_back(residual, head_scale, gain_head[...], head_grad)
    mixture_grad = dot_turned(residual_grad.astype(jnp.bfloat16), out_whole[...])
    mixture_grad = mixture_grad.astype(jnp.bfloat16).astype(jnp.float32)
    qkv_grad = depth_attention_back(mixture_grad, mixed, saved)
    normed_grad = dot_turned(qkv_grad, qkv_whole[...]).astype(jnp.bfloat16).astype(jnp.float32)
    inputs_grad = residual_grad + rms_back(inputs, scale, gain_attn[...], normed_grad)
    grads[mp] = sum(slab(inputs_grad, c) for c in range(CB)).astype(jnp.bfloat16)
    for at, peer in enumerate(swap_peers):
        copy = remote(
            grads.at[mp], grads.at[mp], swap_send.at[2, at], swap_recv.at[2, at], (seq, peer)
        )
        copy.start()
        sends.append(copy)

    for at, peer in enumerate(swap_peers):
        remote(
            loss_parts.at[3], loss_parts.at[at], swap_send.at[1, at], swap_recv.at[1, at], (seq, peer)
        ).wait_recv()
    loss_tiles[seq] = loss_parts[0] + loss_parts[1] + loss_parts[2] + loss_parts[3]
    for d in range(1, seq_count):
        copy = remote(
            loss_tiles.at[seq],
            loss_tiles.at[seq],
            tile_send.at[d - 1],
            tile_recv.at[d - 1],
            (lax.rem(seq + d, seq_count), mp),
        )
        copy.start()
        sends.append(copy)

    for at, peer in enumerate(swap_peers):
        remote(
            grads.at[peer], grads.at[peer], swap_send.at[2, at], swap_recv.at[2, at], (seq, peer)
        ).wait_recv()
    rows = jnp.concatenate([grads[part] for part in range(CB)], axis=0)
    context_grad[...] = dot_turned(rows, proj_whole[...]).astype(jnp.bfloat16)
    for d in range(1, seq_count):
        source = lax.rem(seq + seq_count - d, seq_count)
        remote(
            loss_tiles.at[source],
            loss_tiles.at[source],
            tile_send.at[d - 1],
            tile_recv.at[d - 1],
            (source, mp),
        ).wait_recv()
    losses[...] = loss_tiles[...]
    for copy in sends:
        copy.wait_send()


def whole_step(
    query_states,
    key_states,
    value_states,
    lengths,
    tokens,
    assignment,
    proj_weight,
    query_weight,
    key_weight,
    value_weight,
    out_weight,
    logit_weight,
    embedding,
    gain_attn,
    gain_head,
):
    seq_count, mp_count = lax.axis_size("seq"), lax.axis_size("mp")
    seq_index, mp_index = lax.axis_index("seq"), lax.axis_index("mp")
    frame_count, local_width = query_states.shape
    share = frame_count // mp_count
    slot_cap = 2 * frame_count
    bucket = slot_cap // seq_count
    model_width = proj_weight.shape[1]
    line = seq_count // 2
    slots = (line - 1) + line + 3 * (2 * line - 1)
    vmem = pl.BlockSpec(memory_space=pltpu.VMEM)
    shard = pl.BlockSpec(memory_space=pl.ANY)
    depth_width = 3 * query_weight.shape[1]
    context, context_grad, tiles = pl.pallas_call(
        functools.partial(whole_kernel, line, bucket),
        out_shape=(
            jax.ShapeDtypeStruct((frame_count, local_width), jnp.bfloat16),
            jax.ShapeDtypeStruct((frame_count, local_width), jnp.bfloat16),
            jax.ShapeDtypeStruct((seq_count, seq_count, 128), jnp.float32),
        ),
        in_specs=[pl.BlockSpec(memory_space=pltpu.SMEM)] + [vmem] * 4 + [shard] * 10,
        out_specs=(vmem, vmem, vmem),
        scratch_shapes=[
            pltpu.VMEM((proj_weight.shape[0] * seq_count, model_width), jnp.bfloat16),
            pltpu.VMEM((embedding.shape[0] * seq_count, model_width), jnp.bfloat16),
            pltpu.VMEM((query_weight.shape[0] * seq_count, depth_width), jnp.bfloat16),
            pltpu.VMEM((out_weight.shape[0] * seq_count, model_width), jnp.bfloat16),
            pltpu.VMEM((logit_weight.shape[0] * seq_count, logit_weight.shape[1]), jnp.bfloat16),
            pltpu.VMEM((mp_count, share, model_width), jnp.bfloat16),
            pltpu.VMEM((mp_count - 1, share, model_width), jnp.bfloat16),
            pltpu.VMEM((mp_count, share, model_width), jnp.bfloat16),
            pltpu.VMEM((mp_count, seq_count, 128), jnp.float32),
            pltpu.VMEM((seq_count, seq_count, 128), jnp.float32),
            pltpu.VMEM((frame_count, local_width), jnp.bfloat16),
            pltpu.VMEM((frame_count, local_width), jnp.bfloat16),
            pltpu.VMEM((frame_count, local_width), jnp.bfloat16),
            pltpu.SemaphoreType.DMA((5, slots)),
            pltpu.SemaphoreType.DMA((5, slots)),
            pltpu.SemaphoreType.DMA((10,)),
            pltpu.SemaphoreType.DMA((3, mp_count - 1)),
            pltpu.SemaphoreType.DMA((3, mp_count - 1)),
            pltpu.SemaphoreType.DMA((seq_count - 1,)),
            pltpu.SemaphoreType.DMA((seq_count - 1,)),
        ],
        compiler_params=pltpu.CompilerParams(
            collective_id=0, has_side_effects=True, vmem_limit_bytes=60 * 1024 * 1024
        ),
    )(
        lengths,
        tokens,
        assignment[None, :],
        gain_attn[None, :],
        gain_head[None, :],
        query_states,
        key_states,
        value_states,
        proj_weight,
        query_weight,
        key_weight,
        value_weight,
        out_weight,
        logit_weight,
        embedding,
    )
    sources = slot_cap // mp_count // bucket
    mine = lax.dynamic_slice(
        tiles, (mp_index * sources, seq_index, 0), (sources, 1, bucket)
    )
    return (context, context_grad, mine.reshape(-1))


def fits(query_states, proj_weight, embedding, out_weight):
    seq_count = lax.axis_size("seq")
    return (
        seq_count == 8
        and lax.axis_size("mp") == 4
        and query_states.shape[0] % 128 == 0
        and proj_weight.shape[0] % 16 == 0
        and embedding.shape[0] % 64 == 0
        and out_weight.shape[0] % 64 == 0
    )


def gather_all(*shards):
    return tuple(lax.all_gather(part, "seq", axis=0, tiled=True) for part in shards)


def body(
    query_states,
    key_states,
    value_states,
    lengths,
    tokens,
    assignment,
    proj_weight,
    query_weight,
    key_weight,
    value_weight,
    out_weight,
    logit_weight,
    embedding,
    gain_attn,
    gain_head,
):
    if fits(query_states, proj_weight, embedding, out_weight):
        return whole_step(
            query_states,
            key_states,
            value_states,
            lengths,
            tokens,
            assignment,
            proj_weight,
            query_weight,
            key_weight,
            value_weight,
            out_weight,
            logit_weight,
            embedding,
            gain_attn,
            gain_head,
        )
    seq_index = lax.axis_index("seq")
    frame_count = query_states.shape[0]
    local_width = query_states.shape[1]
    head_count = local_width // HEAD_T
    length = lengths[seq_index]
    places = jnp.arange(frame_count)
    visible = (places[None, :] <= places[:, None]).astype(jnp.float32)
    key_shape = (frame_count, head_count, HEAD_T)
    scores = jnp.einsum(
        "qhd,khd->hqk",
        query_states.reshape(key_shape),
        key_states.reshape(key_shape),
        preferred_element_type=jnp.float32,
    ) / math.sqrt(HEAD_T)
    weights = jnp.exp(scores) * visible[None, :, :]
    totals = jnp.sum(weights, axis=-1)
    mixture = jnp.einsum(
        "hqk,khd->qhd",
        weights.astype(jnp.bfloat16),
        value_states.reshape(key_shape),
        preferred_element_type=jnp.float32,
    )
    mixture = mixture / jnp.transpose(totals)[:, :, None]
    live_mask = (places < length).astype(jnp.float32)
    context = (mixture.reshape(frame_count, local_width) * live_mask[:, None]).astype(jnp.bfloat16)
    proj_quarter, embed_full, qkv_full, out_full, logit_full = gather_all(
        proj_weight,
        embedding,
        jnp.concatenate([query_weight, key_weight, value_weight], axis=1),
        out_weight,
        logit_weight,
    )
    query_full, key_full, value_full = jnp.split(qkv_full, 3, axis=1)
    mp_count = lax.axis_size("mp")
    mp_index = lax.axis_index("mp")
    share = frame_count // mp_count
    first = mp_index * share
    partial_proj = jnp.dot(context, proj_quarter, preferred_element_type=jnp.float32)
    parts = lax.all_to_all(
        partial_proj.astype(jnp.bfloat16).reshape(mp_count, share, -1),
        "mp",
        split_axis=0,
        concat_axis=0,
    )
    hidden = jnp.sum(parts.astype(jnp.float32), axis=0).astype(jnp.bfloat16)
    own_tokens = lax.dynamic_slice_in_dim(tokens, first, share)
    own_live = lax.dynamic_slice_in_dim(live_mask, first, share)

    def total_loss(hidden_in):
        per_frame = depth_losses(
            hidden_in,
            own_tokens,
            own_live,
            query_full,
            key_full,
            value_full,
            out_full,
            logit_full,
            embed_full,
            gain_attn,
            gain_head,
        )
        return (jnp.sum(per_frame), per_frame)

    summed, pullback, own_loss = jax.vjp(total_loss, hidden, has_aux=True)
    hidden_grad = pullback(jnp.ones((), jnp.float32))[0]
    hidden_rows = lax.all_gather(hidden_grad, "mp", axis=0, tiled=True)
    context_grad = jnp.dot(hidden_rows, proj_quarter.T, preferred_element_type=jnp.float32).astype(
        jnp.bfloat16
    )
    frame_loss = lax.all_gather(own_loss, ("seq", "mp"), axis=0, tiled=True)
    frame_slot = lax.all_gather(assignment, "seq", axis=0, tiled=True)
    slot_count = 2 * share
    slots = (seq_index * mp_count + mp_index) * slot_count + jnp.arange(slot_count)
    slot_loss = jnp.sum(
        jnp.where(frame_slot[None, :] == slots[:, None], frame_loss[None, :], 0.0), axis=1
    )
    return (context, context_grad, slot_loss)


def solution(mesh):
    placed = (
        P("seq", "mp"),
        P("seq", "mp"),
        P("seq", "mp"),
        P(),
        P("seq", None),
        P("seq"),
        P(("mp", "seq"), None),
        P("seq", None),
        P("seq", None),
        P("seq", None),
        P("seq", None),
        P("seq", None),
        P("seq", None),
        P(),
        P(),
    )
    return jax.shard_map(
        body,
        mesh=mesh,
        in_specs=placed,
        out_specs=(P("seq", "mp"), P("seq", "mp"), P(("seq", "mp"))),
        check_vma=False,
    )
```
